32 devices in a mesh: groups: 2 (over x), path: 8 (over z, y), cons: 2 (over core).
Axes of the slice: x: 2, y: 2, z: 4, core: 2. Of those that a mesh axis runs over, the one named last changes fastest.
Arguments:
- tile_values: bfloat16 [16, 2, 32, 128, 128], P(('groups', 'path'), 'cons'), parts along dimension 0, may hold values from -0.125 to 0.125
- row_blocks: int32 [16, 2, 32], P(('groups', 'path'), 'cons'), parts along dimension 0, may hold values from 0 to 15, as said below
- col_blocks: int32 [16, 2, 32], P(('groups', 'path'), 'cons'), parts along dimension 0, may hold values from 0 to 7
- path_cost: float32 [16384], P(('groups', 'path', 'cons')), parts along dimension 0, may hold values from -6 to 6
- path_bound: float32 [16384], P(('groups', 'path', 'cons')), parts along dimension 0, may hold values from 0.5 to 2
- primal_start: float32 [16384], P(('groups', 'path', 'cons')), parts along dimension 0, may hold values from 0 to 1
- dual_start: float32 [8192], P(('groups', 'path', 'cons')), parts along dimension 0, may hold values from 0 to 1
- row_limits: float32 [8192], P(('groups', 'path', 'cons')), parts along dimension 0, may hold values from -6 to 6
- step_size: float32 [2], P('groups'), parts along dimension 0, may hold values from 0.3 to 0.45
- weight_start: float32 [2], P('groups'), parts along dimension 0, may hold values from 0.5 to 2
- restart_flags: int32 [12], P('groups'), parts along dimension 0, may hold values from 0 to 1
Outputs:
- primal_out: float32 [16384], P(('groups', 'path', 'cons')), parts along dimension 0
- dual_out: float32 [8192], P(('groups', 'path', 'cons')), parts along dimension 0
- link_loads: float32 [8192], P(('groups', 'path', 'cons')), parts along dimension 0
The draws below stay inside these ranges and needn't reach their ends.
There are 2 independent parts, one for each index of `groups`. The reference program is written for one: setup_inputs(seed, part) draws one part's arguments, and reference() takes and returns one part's arrays. A program takes and returns all parts, laid end to end along the dimension named above; each array names one. Nothing has to cross between parts.
Inputs may be any that keep to these rules, and one draw needn't show every extreme that they name: `row_blocks`: row block of a tile inside its constraint half; for every device and every index o of path, at most 8 of the device's tiles lie in row blocks 2 * o to 2 * o + 1, and on every device some index o has exactly 8.
All inputs are finite; a program needn't handle non-finite values.
Results may differ from the reference program's by a relative error of at most 0.0031.
Values may be sent and summed in bfloat16 or wider, within the bound.
A program may use at most 64 MiB of HBM per device.

```python
import math
import jax
import jax.numpy as jnp
from jax import lax

TILE = 128
CBD = 8
ITERS = 6
RBD = 2
TPD = 32
RB = 16
CAP = 8
NCOL = 8192
NROW = 4096
N_PATH = 8
N_CONS = 2


def device_rows(key):
    keys = jax.random.split(key, 4)
    first = jax.random.randint(keys[0], (), 0, N_PATH).astype(jnp.int32)
    order = jax.random.permutation(keys[1], (N_PATH - 1) * CAP)[:TPD - CAP].astype(jnp.int32)
    others = (order // CAP + first + 1) % N_PATH
    owners = jnp.concatenate([jnp.full((CAP,), first, jnp.int32), others.astype(jnp.int32)])
    owners = owners[jax.random.permutation(keys[2], TPD)]
    inner = jax.random.randint(keys[3], (TPD,), 0, RBD).astype(jnp.int32)
    return (owners * RBD + inner).astype(jnp.int32)


def draw_row_blocks(key, part):
    keys = jax.random.split(jax.random.fold_in(key, 11), N_PATH * N_CONS)
    rows = jax.vmap(device_rows)(keys)
    return rows.reshape(N_PATH, N_CONS, TPD).astype(jnp.int32)


def place_ends(values, own_key, least, largest):
    longest = values.shape.index(max(values.shape))
    spots = []
    for shift in (0, 1):
        where = [jax.random.randint(jax.random.fold_in(own_key, axis), (), 0, length) for axis, length in enumerate(values.shape)]
        where[longest] = (where[longest] + shift) % values.shape[longest]
        spots.append(tuple(where))
    return values.at[spots[0]].set(least).at[spots[1]].set(largest)


def block_levels(stream_key, shape, shards, low, largest):
    level = 1.0
    for axis_at, parts in shards:
        heights = jax.random.uniform(jax.random.fold_in(jax.random.fold_in(stream_key, 6), axis_at), (parts,), jnp.float32, low / len(shards), largest / len(shards))
        level = level * jnp.repeat(jnp.exp(heights), shape[axis_at] // parts).reshape((-1,) + (1,) * (len(shape) - 1 - axis_at))
    return level


def centred(stream_key, extent, scale, reach, cuts=(), kind=jnp.bfloat16):
    array = scale * jax.random.normal(stream_key, extent, jnp.float32)
    if cuts:
        array = array * block_levels(stream_key, extent, cuts, -0.22, 0.18)
    return jnp.clip(array, -reach, reach).astype(kind)


def setup_inputs(seed: int = 0, part: int = 0) -> dict:
    key_list = jax.random.split(jax.random.key(seed), 12)
    own_keys = jax.random.split(jax.random.fold_in(key_list[11], part), 12)
    return {
        "tile_values": centred(own_keys[0], (N_PATH, N_CONS, TPD, TILE, TILE), (TILE * TPD // RBD) ** -0.5, 0.125, ((0, 8), (1, 2))),
        "row_blocks": draw_row_blocks(jax.random.fold_in(jax.random.fold_in(key_list[11], part), 71), part),
        "col_blocks": place_ends(jax.random.randint(own_keys[2], (N_PATH, N_CONS, TPD), 0, CBD), jax.random.fold_in(own_keys[2], 1), 0, CBD - 1).astype(jnp.int32),
        "path_cost": centred(own_keys[3], (NCOL,), 1.0, 6.0, ((0, 16),), jnp.float32),
        "path_bound": jnp.clip(0.5 + 1.5 * jax.random.uniform(own_keys[4], (NCOL,), jnp.float32) ** block_levels(own_keys[4], (NCOL,), ((0, 16),), -0.2, 0.2), 0.5, 2.0),
        "primal_start": jnp.clip(1.0 * jax.random.uniform(own_keys[5], (NCOL,), jnp.float32) ** block_levels(own_keys[5], (NCOL,), ((0, 16),), -0.2, 0.2), 0.0, 1.0),
        "dual_start": jnp.clip(1.0 * jax.random.uniform(own_keys[6], (NROW,), jnp.float32) ** block_levels(own_keys[6], (NROW,), ((0, 16),), -0.2, 0.2), 0.0, 1.0),
        "row_limits": centred(own_keys[7], (NROW,), 1.0, 6.0, ((0, 16),), jnp.float32),
        "step_size": jnp.clip(jax.random.uniform(own_keys[8], (1,), jnp.float32, 0.3, 0.45), 0.3, 0.45),
        "weight_start": jnp.clip(jnp.exp(jax.random.uniform(own_keys[9], (1,), jnp.float32, math.log(0.5), math.log(2.0))), 0.5, 2.0),
        "restart_flags": place_ends(jax.random.randint(own_keys[10], (ITERS,), 0, 2), jax.random.fold_in(own_keys[10], 1), 0, 1).astype(jnp.int32),
    }


def to_halves(vector):
    return vector.reshape(N_PATH, N_CONS, -1).transpose(1, 0, 2).reshape(N_CONS, -1)

def from_halves(halves):
    return halves.reshape(N_CONS, N_PATH, -1).transpose(1, 0, 2).reshape(-1)

def row_activity(tile_values, row_blocks, col_blocks, primal_low):

    def per_path(items):
        tiles_here, rows_here, cols_here, primal_here = items
        blocks = primal_here.reshape(CBD, TILE).astype(jnp.float32)
        pieces = []
        for half in range(N_CONS):
            picked = blocks[cols_here[half]]
            products = jnp.einsum('tij,tj->ti', tiles_here[half].astype(jnp.float32), picked)
            pieces.append(jax.ops.segment_sum(products, rows_here[half], num_segments=RB).reshape(-1))
        return jnp.stack(pieces)
    terms = lax.map(per_path, (tile_values, row_blocks, col_blocks, primal_low.reshape(N_PATH, -1)))
    return from_halves(lax.optimization_barrier(jnp.sum(terms, axis=0)))

def col_activity(tile_values, row_blocks, col_blocks, dual_low):
    halves = to_halves(dual_low)

    def per_path(items):
        tiles_here, rows_here, cols_here = items
        total = jnp.zeros((CBD * TILE,), jnp.float32)
        for half in range(N_CONS):
            blocks = halves[half].reshape(RB, TILE).astype(jnp.float32)
            picked = blocks[rows_here[half]]
            products = jnp.einsum('tij,ti->tj', tiles_here[half].astype(jnp.float32), picked)
            total = total + jax.ops.segment_sum(products, cols_here[half], num_segments=CBD).reshape(-1)
        return total
    terms = lax.map(per_path, (tile_values, row_blocks, col_blocks))
    return terms.reshape(-1)

def reference(tile_values, row_blocks, col_blocks, path_cost, path_bound, primal_start, dual_start, row_limits, step_size, weight_start, restart_flags):
    epsilon = 1e-06
    primal_now = primal_start
    dual_now = dual_start
    anchor_primal = primal_now
    anchor_dual = dual_now
    primal_sum = jnp.zeros_like(primal_now)
    dual_sum = jnp.zeros_like(dual_now)
    steps_taken = jnp.zeros((), jnp.float32)
    eta = step_size[0]
    weight = weight_start[0]
    for turn_index in range(ITERS):
        gradient = col_activity(tile_values, row_blocks, col_blocks, dual_now.astype(jnp.bfloat16))
        primal_next = jnp.clip(primal_now - eta / weight * (path_cost + gradient), 0.0, path_bound)
        extrapolated = (2.0 * primal_next - primal_now).astype(jnp.bfloat16)
        activity = row_activity(tile_values, row_blocks, col_blocks, extrapolated)
        dual_next = jnp.maximum(dual_now + eta * weight * (activity - row_limits), 0.0)
        primal_sum = primal_sum + primal_next
        dual_sum = dual_sum + dual_next
        steps_taken = steps_taken + 1.0
        primal_mean = primal_sum / steps_taken
        dual_mean = dual_sum / steps_taken
        primal_move = jnp.sum((primal_mean - anchor_primal) ** 2)
        dual_move = jnp.sum((dual_mean - anchor_dual) ** 2)
        candidate = jnp.sqrt(weight * jnp.sqrt(dual_move + epsilon) / jnp.sqrt(primal_move + epsilon))
        restart = restart_flags[turn_index] == 1
        primal_now = jnp.where(restart, primal_mean, primal_next)
        dual_now = jnp.where(restart, dual_mean, dual_next)
        anchor_primal = jnp.where(restart, primal_mean, anchor_primal)
        anchor_dual = jnp.where(restart, dual_mean, anchor_dual)
        primal_sum = jnp.where(restart, jnp.zeros_like(primal_sum), primal_sum)
        dual_sum = jnp.where(restart, jnp.zeros_like(dual_sum), dual_sum)
        steps_taken = jnp.where(restart, jnp.zeros((), jnp.float32), steps_taken)
        weight = jnp.where(restart, candidate, weight)
    link_loads = row_activity(tile_values, row_blocks, col_blocks, primal_now.astype(jnp.bfloat16))
    return (primal_now, dual_now, link_loads)
```

```python
import functools
import jax
import jax.numpy as jnp
from jax import lax
from jax.experimental import pallas as pl
from jax.experimental.pallas import tpu as pltpu
from jax.sharding import PartitionSpec as P

LANES = 128
EPSILON = 1e-06


def kernel(
    n,
    iters,
    tiles_hbm,
    rows_s,
    cols_s,
    cost_in,
    bound_in,
    primal_in,
    dual_in,
    limits_in,
    step_s,
    weight_s,
    flags_s,
    primal_out,
    dual_out,
    loads_out,
    tiles,
    turned,
    start_buf,
    flows,
    dual_buf,
    grad_out,
    grad_in,
    act_out,
    act_in,
    tile_sem,
    start_send,
    start_recv,
    dual_send,
    dual_recv,
    grad_send,
    grad_recv,
    act_send,
    act_recv,
):
    me = lax.axis_index("path")
    core = lax.axis_index("cons")
    other = 1 - core
    count = tiles.shape[0]
    half = cost_in.shape[0]
    own = dual_in.shape[0]
    blocks = 2 * half
    unroll = n <= 8

    def peers(body):
        def step(k, carry):
            body(lax.rem(me + k, n))
            return carry

        lax.fori_loop(1, n, step, 0, unroll=unroll)

    tile_copy = pltpu.make_async_copy(tiles_hbm.at[0, 0], tiles, tile_sem)
    tile_copy.start()
    barrier = pltpu.get_barrier_semaphore()
    peers(lambda q: pl.semaphore_signal(barrier, inc=1, device_id={"path": q}))
    pl.semaphore_signal(barrier, inc=1, device_id={"cons": other})

    start_buf[core, 0] = cost_in[...]
    start_buf[core, 1] = bound_in[...]
    start_buf[core, 2] = primal_in[...]
    dual_buf[me, pl.ds(0, own)] = dual_in[...]
    dual_buf[me, pl.ds(own, 2)] = jnp.zeros((2, LANES), jnp.float32)
    pl.semaphore_wait(barrier, n)

    def dual_copy(source, q):
        return pltpu.make_async_remote_copy(
            src_ref=dual_buf.at[source],
            dst_ref=dual_buf.at[source],
            send_sem=dual_send.at[q],
            recv_sem=dual_recv.at[source],
            device_id={"path": q},
        )

    def act_copy(source, q, rows):
        return pltpu.make_async_remote_copy(
            src_ref=act_out.at[q, pl.ds(0, rows)],
            dst_ref=act_in.at[source, pl.ds(0, rows)],
            send_sem=act_send.at[q],
            recv_sem=act_recv.at[source],
            device_id={"path": q},
        )

    def grad_copy(slot):
        return pltpu.make_async_remote_copy(
            src_ref=grad_out.at[slot],
            dst_ref=grad_in.at[slot],
            send_sem=grad_send.at[slot],
            recv_sem=grad_recv.at[slot],
            device_id={"cons": other},
        )

    def start_copy(slot):
        return pltpu.make_async_remote_copy(
            src_ref=start_buf.at[slot],
            dst_ref=start_buf.at[slot],
            send_sem=start_send,
            recv_sem=start_recv,
            device_id={"cons": other},
        )

    peers(lambda q: dual_copy(me, q).start())
    start_copy(core).start()
    tile_copy.wait()
    for t in range(count):
        turned[t] = tiles[t].T
    start_copy(other).wait_recv()

    def whole(item):
        return jnp.concatenate([start_buf[0, item], start_buf[1, item]], axis=0)

    cost, bound, primal = whole(0), whole(1), whole(2)
    start_copy(core).wait_send()
    dual = dual_in[...]
    limits = limits_in[...]
    eta = step_s[0]
    weight = jnp.full((1, LANES), weight_s[0], jnp.float32)
    anchor_primal, anchor_dual = primal, dual
    primal_sum, dual_sum = jnp.zeros_like(primal), jnp.zeros_like(dual)
    taken = jnp.zeros((1, LANES), jnp.float32)
    col_iota = lax.broadcasted_iota(jnp.int32, (blocks, LANES), 0)

    for turn in range(iters):
        slot = turn % 2
        last = turn == iters - 1
        peers(lambda q: dual_copy(q, q).wait_recv())
        parts = []
        for t in range(count):
            row = rows_s[t]
            line = dual_buf[row // own, pl.ds(row % own, 1)]
            parts.append(jnp.where(col_iota == cols_s[t], line, 0.0).astype(jnp.bfloat16))
        left = jnp.concatenate(parts, axis=1)
        partial = jnp.dot(
            left, tiles[...].reshape(count * LANES, LANES), preferred_element_type=jnp.float32
        )
        if turn >= 2:
            grad_copy(slot).wait_send()
        grad_out[slot, pl.ds(0, blocks)] = partial
        moves = jnp.sum(dual_buf[:, own, :], axis=0, keepdims=True)
        grad_out[slot, pl.ds(blocks, 8)] = jnp.broadcast_to(moves, (8, LANES))
        grad_copy(slot).start()
        primal_moves = jnp.sum(dual_buf[:, own + 1, :], axis=0, keepdims=True)
        primal_move = jnp.sum(primal_moves, axis=1, keepdims=True)
        grad_copy(slot).wait_recv()
        gradient = partial + grad_in[slot, pl.ds(0, blocks)]
        if turn > 0:
            moves = moves + grad_in[slot, pl.ds(blocks, 1)]
            dual_move = jnp.sum(moves, axis=1, keepdims=True)
            candidate = jnp.sqrt(
                weight * jnp.sqrt(dual_move + EPSILON) / jnp.sqrt(primal_move + EPSILON)
            )
            weight = jnp.where(flags_s[turn - 1] == 1, candidate, weight)
        restart = flags_s[turn] == 1
        primal_next = jnp.clip(primal - eta / weight * (cost + gradient), 0.0, bound)
        extrapolated = 2.0 * primal_next - primal
        primal_sum = primal_sum + primal_next
        taken = taken + 1.0
        primal_mean = primal_sum / taken
        shift = primal_mean - anchor_primal
        primal_part = jnp.sum(shift * shift, axis=0, keepdims=True)
        primal = jnp.where(restart, primal_mean, primal_next)
        anchor_primal = jnp.where(restart, primal_mean, anchor_primal)
        primal_sum = jnp.where(restart, 0.0, primal_sum)

        rows = 2 * own if last else own
        row_iota = lax.broadcasted_iota(jnp.int32, (n * rows, LANES), 0)
        parts = []
        lines = [extrapolated, primal] if last else [extrapolated]
        if turn > 0:
            peers(lambda q: act_copy(me, q, own).wait_send())
        for index, line in enumerate(lines):
            flows[index] = line
        for t in range(count):
            row, col = rows_s[t], cols_s[t]
            spot = (row // own) * rows + row % own
            piece = jnp.zeros((n * rows, LANES), jnp.float32)
            for index in range(len(lines)):
                line = flows[index, pl.ds(col, 1)]
                piece = jnp.where(row_iota == spot + index * own, line, piece)
            parts.append(piece.astype(jnp.bfloat16))
        left = jnp.concatenate(parts, axis=1)
        activity = jnp.dot(
            left, turned[...].reshape(count * LANES, LANES), preferred_element_type=jnp.float32
        )
        for q in range(n):
            act_out[q, pl.ds(0, rows)] = activity[q * rows : (q + 1) * rows]
        peers(lambda q: act_copy(me, q, rows).start())
        act_in[me, pl.ds(0, rows)] = act_out[me, pl.ds(0, rows)]
        peers(lambda q: dual_copy(me, q).wait_send())
        peers(lambda q: act_copy(q, q, rows).wait_recv())
        total = jnp.sum(act_in[:, pl.ds(0, rows)], axis=0)
        dual_next = jnp.maximum(dual + eta * weight * (total[:own] - limits), 0.0)
        dual_sum = dual_sum + dual_next
        dual_mean = dual_sum / taken
        shift = dual_mean - anchor_dual
        dual = jnp.where(restart, dual_mean, dual_next)
        anchor_dual = jnp.where(restart, dual_mean, anchor_dual)
        dual_sum = jnp.where(restart, 0.0, dual_sum)
        taken = jnp.where(restart, 0.0, taken)
        if not last:
            dual_buf[me, pl.ds(0, own)] = dual
            dual_buf[me, pl.ds(own, 1)] = jnp.sum(shift * shift, axis=0, keepdims=True)
            dual_buf[me, pl.ds(own + 1, 1)] = primal_part
            peers(lambda q: dual_copy(me, q).start())

    primal_out[...] = jnp.where(core == 0, primal[:half], primal[half:])
    dual_out[...] = dual
    loads_out[...] = total[own:]
    peers(lambda q: act_copy(me, q, 2 * own).wait_send())
    for turn in range(max(iters - 2, 0), iters):
        grad_copy(turn % 2).wait_send()


def shards(
    tile_values,
    row_blocks,
    col_blocks,
    path_cost,
    path_bound,
    primal_start,
    dual_start,
    row_limits,
    step_size,
    weight_start,
    restart_flags,
):
    n = lax.axis_size("path")
    count = row_blocks.shape[2]
    half = path_cost.shape[0] // LANES
    own = dual_start.shape[0] // LANES
    vmem = pl.BlockSpec(memory_space=pltpu.VMEM)
    smem = pl.BlockSpec(memory_space=pltpu.SMEM)
    dma = pltpu.SemaphoreType.DMA
    primal, dual, loads = pl.pallas_call(
        functools.partial(kernel, n, restart_flags.shape[0]),
        out_shape=(
            jax.ShapeDtypeStruct((half, LANES), jnp.float32),
            jax.ShapeDtypeStruct((own, LANES), jnp.float32),
            jax.ShapeDtypeStruct((own, LANES), jnp.float32),
        ),
        in_specs=[
            pl.BlockSpec(memory_space=pl.ANY),
            smem,
            smem,
            vmem,
            vmem,
            vmem,
            vmem,
            vmem,
            smem,
            smem,
            smem,
        ],
        out_specs=(vmem, vmem, vmem),
        scratch_shapes=[
            pltpu.VMEM((count, LANES, LANES), jnp.bfloat16),
            pltpu.VMEM((count, LANES, LANES), jnp.bfloat16),
            pltpu.VMEM((2, 3, half, LANES), jnp.float32),
            pltpu.VMEM((2, 2 * half, LANES), jnp.float32),
            pltpu.VMEM((n, own + 2, LANES), jnp.float32),
            pltpu.VMEM((2, 2 * half + 8, LANES), jnp.float32),
            pltpu.VMEM((2, 2 * half + 8, LANES), jnp.float32),
            pltpu.VMEM((n, 2 * own, LANES), jnp.float32),
            pltpu.VMEM((n, 2 * own, LANES), jnp.float32),
            dma,
            dma,
            dma,
            dma((n,)),
            dma((n,)),
            dma((2,)),
            dma((2,)),
            dma((n,)),
            dma((n,)),
        ],
        compiler_params=pltpu.CompilerParams(
            collective_id=0, has_side_effects=True, vmem_limit_bytes=32 * 1024 * 1024
        ),
    )(
        tile_values,
        row_blocks.reshape(count),
        col_blocks.reshape(count),
        path_cost.reshape(half, LANES),
        path_bound.reshape(half, LANES),
        primal_start.reshape(half, LANES),
        dual_start.reshape(own, LANES),
        row_limits.reshape(own, LANES),
        step_size,
        weight_start,
        restart_flags,
    )
    return (primal.reshape(-1), dual.reshape(-1), loads.reshape(-1))


def solution(mesh):
    in_specs = (
        P(("groups", "path"), "cons", None, None, None),
        P(("groups", "path"), "cons", None),
        P(("groups", "path"), "cons", None),
        P(("groups", "path", "cons")),
        P(("groups", "path", "cons")),
        P(("groups", "path", "cons")),
        P(("groups", "path", "cons")),
        P(("groups", "path", "cons")),
        P("groups"),
        P("groups"),
        P("groups"),
    )
    out_specs = (
        P(("groups", "path", "cons")),
        P(("groups", "path", "cons")),
        P(("groups", "path", "cons")),
    )
    return jax.shard_map(shards, mesh=mesh, in_specs=in_specs, out_specs=out_specs, check_vma=False)
```

```python
import functools
import jax
import jax.numpy as jnp
from jax import lax
from jax.experimental import pallas as pl
from jax.experimental.pallas import tpu as pltpu
from jax.sharding import PartitionSpec as P

LANES = 128
EPSILON = 1e-06


def kernel(
    n,
    iters,
    tiles_hbm,
    rows_s,
    cols_s,
    cost_in,
    bound_in,
    primal_in,
    dual_in,
    limits_in,
    step_s,
    weight_s,
    flags_s,
    primal_out,
    dual_out,
    loads_out,
    tiles,
    turned,
    start_buf,
    flows,
    dual_buf,
    dual_all,
    limit_all,
    grad_out,
    grad_in,
    act_all,
    act_out,
    act_in,
    tile_sem,
    start_send,
    start_recv,
    dual_send,
    dual_recv,
    grad_send,
    grad_recv,
    all_send,
    all_recv,
    act_send,
    act_recv,
):
    me = lax.axis_index("path")
    core = lax.axis_index("cons")
    other = 1 - core
    count = tiles.shape[0]
    half = cost_in.shape[0]
    own = dual_in.shape[0]
    blocks = 2 * half
    unroll = n <= 8

    def peers(body):
        def step(k, carry):
            body(lax.rem(me + k, n))
            return carry

        lax.fori_loop(1, n, step, 0, unroll=unroll)

    tile_copy = pltpu.make_async_copy(tiles_hbm.at[0, 0], tiles, tile_sem)
    tile_copy.start()
    barrier = pltpu.get_barrier_semaphore()
    peers(lambda q: pl.semaphore_signal(barrier, inc=1, device_id={"path": q}))
    pl.semaphore_signal(barrier, inc=1, device_id={"cons": other})

    start_buf[core, 0] = cost_in[...]
    start_buf[core, 1] = bound_in[...]
    start_buf[core, 2] = primal_in[...]
    dual_buf[me, pl.ds(0, own)] = dual_in[...]
    dual_buf[me, pl.ds(own, own)] = limits_in[...]
    pl.semaphore_wait(barrier, n)

    def dual_copy(source, q):
        return pltpu.make_async_remote_copy(
            src_ref=dual_buf.at[source],
            dst_ref=dual_buf.at[source],
            send_sem=dual_send.at[q],
            recv_sem=dual_recv.at[source],
            device_id={"path": q},
        )

    def all_copy(slot, source, q):
        return pltpu.make_async_remote_copy(
            src_ref=act_all.at[slot, source],
            dst_ref=act_all.at[slot, source],
            send_sem=all_send.at[slot, q],
            recv_sem=all_recv.at[slot, source],
            device_id={"path": q},
        )

    def act_copy(source, q):
        return pltpu.make_async_remote_copy(
            src_ref=act_out.at[q],
            dst_ref=act_in.at[source],
            send_sem=act_send.at[q],
            recv_sem=act_recv.at[source],
            device_id={"path": q},
        )

    def grad_copy(slot):
        return pltpu.make_async_remote_copy(
            src_ref=grad_out.at[slot],
            dst_ref=grad_in.at[slot],
            send_sem=grad_send.at[slot],
            recv_sem=grad_recv.at[slot],
            device_id={"cons": other},
        )

    def start_copy(slot):
        return pltpu.make_async_remote_copy(
            src_ref=start_buf.at[slot],
            dst_ref=start_buf.at[slot],
            send_sem=start_send,
            recv_sem=start_recv,
            device_id={"cons": other},
        )

    peers(lambda q: dual_copy(me, q).start())
    start_copy(core).start()
    tile_copy.wait()
    for t in range(count):
        turned[t] = tiles[t].T
    start_copy(other).wait_recv()

    def whole(item):
        return jnp.concatenate([start_buf[0, item], start_buf[1, item]], axis=0)

    cost, bound, primal = whole(0), whole(1), whole(2)
    start_copy(core).wait_send()
    peers(lambda q: dual_copy(q, q).wait_recv())
    for q in range(n):
        dual_all[pl.ds(q * own, own)] = dual_buf[q, pl.ds(0, own)]
        limit_all[pl.ds(q * own, own)] = dual_buf[q, pl.ds(own, own)]
    dual = dual_all[...]
    limits = limit_all[...]
    peers(lambda q: dual_copy(me, q).wait_send())
    moves = jnp.zeros((1, LANES), jnp.float32)
    primal_moves = moves
    eta = step_s[0]
    weight = jnp.full((1, LANES), weight_s[0], jnp.float32)
    anchor_primal, anchor_dual = primal, dual
    primal_sum, dual_sum = jnp.zeros_like(primal), jnp.zeros_like(dual)
    taken = jnp.zeros((1, LANES), jnp.float32)
    col_iota = lax.broadcasted_iota(jnp.int32, (blocks, LANES), 0)

    for turn in range(iters):
        slot = turn % 2
        last = turn == iters - 1
        parts = []
        for t in range(count):
            line = dual_all[pl.ds(rows_s[t], 1)]
            parts.append(jnp.where(col_iota == cols_s[t], line, 0.0).astype(jnp.bfloat16))
        left = jnp.concatenate(parts, axis=1)
        partial = jnp.dot(
            left, tiles[...].reshape(count * LANES, LANES), preferred_element_type=jnp.float32
        )
        if turn >= 2:
            grad_copy(slot).wait_send()
        grad_out[slot, pl.ds(0, blocks)] = partial
        grad_out[slot, pl.ds(blocks, 8)] = jnp.broadcast_to(moves, (8, LANES))
        grad_copy(slot).start()
        primal_move = jnp.sum(primal_moves, axis=1, keepdims=True)
        grad_copy(slot).wait_recv()
        gradient = partial + grad_in[slot, pl.ds(0, blocks)]
        if turn > 0:
            moves = moves + grad_in[slot, pl.ds(blocks, 1)]
            dual_move = jnp.sum(moves, axis=1, keepdims=True)
            candidate = jnp.sqrt(
                weight * jnp.sqrt(dual_move + EPSILON) / jnp.sqrt(primal_move + EPSILON)
            )
            weight = jnp.where(flags_s[turn - 1] == 1, candidate, weight)
        restart = flags_s[turn] == 1
        primal_next = jnp.clip(primal - eta / weight * (cost + gradient), 0.0, bound)
        extrapolated = 2.0 * primal_next - primal
        primal_sum = primal_sum + primal_next
        taken = taken + 1.0
        primal_mean = primal_sum / taken
        shift = primal_mean - anchor_primal
        primal_part = jnp.sum(shift * shift, axis=0, keepdims=True)
        primal = jnp.where(restart, primal_mean, primal_next)
        anchor_primal = jnp.where(restart, primal_mean, anchor_primal)
        primal_sum = jnp.where(restart, 0.0, primal_sum)

        rows = 2 * own if last else own
        row_iota = lax.broadcasted_iota(jnp.int32, (n * rows, LANES), 0)
        parts = []
        lines = [extrapolated, primal] if last else [extrapolated]
        for index, line in enumerate(lines):
            flows[index] = line
        for t in range(count):
            row, col = rows_s[t], cols_s[t]
            spot = (row // own) * rows + row % own
            piece = jnp.zeros((n * rows, LANES), jnp.float32)
            for index in range(len(lines)):
                line = flows[index, pl.ds(col, 1)]
                piece = jnp.where(row_iota == spot + index * own, line, piece)
            parts.append(piece.astype(jnp.bfloat16))
        left = jnp.concatenate(parts, axis=1)
        activity = jnp.dot(
            left, turned[...].reshape(count * LANES, LANES), preferred_element_type=jnp.float32
        )
        if last:
            for q in range(n):
                act_out[q] = activity[q * rows : (q + 1) * rows]
            peers(lambda q: act_copy(me, q).start())
            act_in[me] = act_out[me]
            mine = pl.ds(me * own, own)
            dual = dual_all[mine]
            limit_all[...] = dual_sum
            dual_sum = limit_all[mine]
            peers(lambda q: act_copy(q, q).wait_recv())
            total = jnp.sum(act_in[...], axis=0)
            dual_next = jnp.maximum(dual + eta * weight * (total[:own] - limits_in[...]), 0.0)
            dual = jnp.where(restart, (dual_sum + dual_next) / taken, dual_next)
        else:
            if turn >= 2:
                peers(lambda q: all_copy(slot, me, q).wait_send())
            act_all[slot, me, pl.ds(0, n * own)] = activity
            act_all[slot, me, pl.ds(n * own, 1)] = primal_part
            peers(lambda q: all_copy(slot, me, q).start())
            peers(lambda q: all_copy(slot, q, q).wait_recv())
            total = jnp.sum(act_all[slot, :, pl.ds(0, n * own)], axis=0)
            primal_moves = jnp.sum(act_all[slot, :, n * own, :], axis=0, keepdims=True)
            dual_next = jnp.maximum(dual + eta * weight * (total - limits), 0.0)
            dual_sum = dual_sum + dual_next
            dual_mean = dual_sum / taken
            shift = dual_mean - anchor_dual
            moves = jnp.sum(shift * shift, axis=0, keepdims=True)
            dual = jnp.where(restart, dual_mean, dual_next)
            anchor_dual = jnp.where(restart, dual_mean, anchor_dual)
            dual_sum = jnp.where(restart, 0.0, dual_sum)
            taken = jnp.where(restart, 0.0, taken)
            dual_all[...] = dual

    primal_out[...] = jnp.where(core == 0, primal[:half], primal[half:])
    dual_out[...] = dual
    loads_out[...] = total[own:]
    peers(lambda q: act_copy(me, q).wait_send())
    for turn in range(max(iters - 3, 0), iters - 1):
        peers(functools.partial(lambda slot, q: all_copy(slot, me, q).wait_send(), turn % 2))
    for turn in range(max(iters - 2, 0), iters):
        grad_copy(turn % 2).wait_send()


def shards(
    tile_values,
    row_blocks,
    col_blocks,
    path_cost,
    path_bound,
    primal_start,
    dual_start,
    row_limits,
    step_size,
    weight_start,
    restart_flags,
):
    n = lax.axis_size("path")
    count = row_blocks.shape[2]
    half = path_cost.shape[0] // LANES
    own = dual_start.shape[0] // LANES
    vmem = pl.BlockSpec(memory_space=pltpu.VMEM)
    smem = pl.BlockSpec(memory_space=pltpu.SMEM)
    dma = pltpu.SemaphoreType.DMA
    primal, dual, loads = pl.pallas_call(
        functools.partial(kernel, n, restart_flags.shape[0]),
        out_shape=(
            jax.ShapeDtypeStruct((half, LANES), jnp.float32),
            jax.ShapeDtypeStruct((own, LANES), jnp.float32),
            jax.ShapeDtypeStruct((own, LANES), jnp.float32),
        ),
        in_specs=[
            pl.BlockSpec(memory_space=pl.ANY),
            smem,
            smem,
            vmem,
            vmem,
            vmem,
            vmem,
            vmem,
            smem,
            smem,
            smem,
        ],
        out_specs=(vmem, vmem, vmem),
        scratch_shapes=[
            pltpu.VMEM((count, LANES, LANES), jnp.bfloat16),
            pltpu.VMEM((count, LANES, LANES), jnp.bfloat16),
            pltpu.VMEM((2, 3, half, LANES), jnp.float32),
            pltpu.VMEM((2, 2 * half, LANES), jnp.float32),
            pltpu.VMEM((n, 2 * own, LANES), jnp.float32),
            pltpu.VMEM((n * own, LANES), jnp.float32),
            pltpu.VMEM((n * own, LANES), jnp.float32),
            pltpu.VMEM((2, 2 * half + 8, LANES), jnp.float32),
            pltpu.VMEM((2, 2 * half + 8, LANES), jnp.float32),
            pltpu.VMEM((2, n, n * own + 1, LANES), jnp.float32),
            pltpu.VMEM((n, 2 * own, LANES), jnp.float32),
            pltpu.VMEM((n, 2 * own, LANES), jnp.float32),
            dma,
            dma,
            dma,
            dma((n,)),
            dma((n,)),
            dma((2,)),
            dma((2,)),
            dma((2, n)),
            dma((2, n)),
            dma((n,)),
            dma((n,)),
        ],
        compiler_params=pltpu.CompilerParams(
            collective_id=0, has_side_effects=True, vmem_limit_bytes=32 * 1024 * 1024
        ),
    )(
        tile_values,
        row_blocks.reshape(count),
        col_blocks.reshape(count),
        path_cost.reshape(half, LANES),
        path_bound.reshape(half, LANES),
        primal_start.reshape(half, LANES),
        dual_start.reshape(own, LANES),
        row_limits.reshape(own, LANES),
        step_size,
        weight_start,
        restart_flags,
    )
    return (primal.reshape(-1), dual.reshape(-1), loads.reshape(-1))


def solution(mesh):
    in_specs = (
        P(("groups", "path"), "cons", None, None, None),
        P(("groups", "path"), "cons", None),
        P(("groups", "path"), "cons", None),
        P(("groups", "path", "cons")),
        P(("groups", "path", "cons")),
        P(("groups", "path", "cons")),
        P(("groups", "path", "cons")),
        P(("groups", "path", "cons")),
        P("groups"),
        P("groups"),
        P("groups"),
    )
    out_specs = (
        P(("groups", "path", "cons")),
        P(("groups", "path", "cons")),
        P(("groups", "path", "cons")),
    )
    return jax.shard_map(shards, mesh=mesh, in_specs=in_specs, out_specs=out_specs, check_vma=False)
```

```python
import functools
import jax
import jax.numpy as jnp
from jax import lax
from jax.experimental import pallas as pl
from jax.experimental.pallas import tpu as pltpu
from jax.sharding import PartitionSpec as P

LANES = 128
EPSILON = 1e-06


def kernel(
    n,
    iters,
    tiles_hbm,
    rows_s,
    cols_s,
    cost_in,
    bound_in,
    primal_in,
    dual_in,
    limits_in,
    step_s,
    weight_s,
    flags_s,
    primal_out,
    dual_out,
    loads_out,
    tiles,
    turned,
    start_buf,
    flows,
    dual_buf,
    dual_all,
    limit_all,
    grad_out,
    grad_in,
    act_all,
    act_out,
    act_in,
    tile_sem,
    fetch_sem,
    start_send,
    start_recv,
    dual_send,
    dual_recv,
    grad_send,
    grad_recv,
    all_send,
    all_recv,
    act_send,
    act_recv,
):
    me = lax.axis_index("path")
    core = lax.axis_index("cons")
    other = 1 - core
    count = tiles.shape[0]
    half = cost_in.shape[0]
    own = dual_in.shape[0]
    blocks = 2 * half
    unroll = n <= 8

    flips = []
    if n == 8:
        bits = [lax.rem(me // (1 << i), 2) for i in range(3)]
        for k in range(7, 0, -1):
            flips.append(me + sum((1 << i) * (1 - 2 * bits[i]) for i in range(3) if k >> i & 1))

    def peers(body):
        def step(k, carry):
            body(lax.rem(me + k, n))
            return carry

        if flips:
            for q in flips:
                body(q)
            return

        lax.fori_loop(1, n, step, 0, unroll=unroll)

    tile_copy = pltpu.make_async_copy(tiles_hbm.at[0, 0], tiles, tile_sem)
    fetches = [
        pltpu.make_async_copy(dual_in, dual_buf.at[me, pl.ds(0, own)], fetch_sem.at[0]),
        pltpu.make_async_copy(limits_in, dual_buf.at[me, pl.ds(own, own)], fetch_sem.at[1]),
        pltpu.make_async_copy(cost_in, start_buf.at[core, 0], fetch_sem.at[2]),
        pltpu.make_async_copy(bound_in, start_buf.at[core, 1], fetch_sem.at[3]),
        pltpu.make_async_copy(primal_in, start_buf.at[core, 2], fetch_sem.at[4]),
    ]
    for copy in fetches:
        copy.start()
    tile_copy.start()
    barrier = pltpu.get_barrier_semaphore()
    peers(lambda q: pl.semaphore_signal(barrier, inc=1, device_id={"path": q}))
    pl.semaphore_signal(barrier, inc=1, device_id={"cons": other})

    for copy in fetches:
        copy.wait()
    pl.semaphore_wait(barrier, n)

    def dual_copy(source, q):
        return pltpu.make_async_remote_copy(
            src_ref=dual_buf.at[source],
            dst_ref=dual_buf.at[source],
            send_sem=dual_send.at[q],
            recv_sem=dual_recv.at[source],
            device_id={"path": q},
        )

    def all_copy(slot, source, q):
        return pltpu.make_async_remote_copy(
            src_ref=act_all.at[slot, source],
            dst_ref=act_all.at[slot, source],
            send_sem=all_send.at[slot, q],
            recv_sem=all_recv.at[slot, source],
            device_id={"path": q},
        )

    def act_copy(source, q):
        return pltpu.make_async_remote_copy(
            src_ref=act_out.at[q],
            dst_ref=act_in.at[source],
            send_sem=act_send.at[q],
            recv_sem=act_recv.at[source],
            device_id={"path": q},
        )

    def grad_copy(slot):
        return pltpu.make_async_remote_copy(
            src_ref=grad_out.at[slot],
            dst_ref=grad_in.at[slot],
            send_sem=grad_send.at[slot],
            recv_sem=grad_recv.at[slot],
            device_id={"cons": other},
        )

    def start_copy(slot):
        return pltpu.make_async_remote_copy(
            src_ref=start_buf.at[slot],
            dst_ref=start_buf.at[slot],
            send_sem=start_send,
            recv_sem=start_recv,
            device_id={"cons": other},
        )

    peers(lambda q: dual_copy(me, q).start())
    start_copy(core).start()
    tile_copy.wait()
    for t in range(count):
        turned[t] = tiles[t].T
    start_copy(other).wait_recv()

    def whole(item):
        return jnp.concatenate([start_buf[0, item], start_buf[1, item]], axis=0)

    cost, bound, primal = whole(0), whole(1), whole(2)
    start_copy(core).wait_send()
    peers(lambda q: dual_copy(q, q).wait_recv())
    for q in range(n):
        dual_all[pl.ds(q * own, own)] = dual_buf[q, pl.ds(0, own)]
        limit_all[pl.ds(q * own, own)] = dual_buf[q, pl.ds(own, own)]
    dual = dual_all[...]
    limits = limit_all[...]
    peers(lambda q: dual_copy(me, q).wait_send())
    moves = jnp.zeros((1, LANES), jnp.float32)
    primal_moves = moves
    eta = step_s[0]
    weight = jnp.full((1, LANES), weight_s[0], jnp.float32)
    anchor_primal, anchor_dual = primal, dual
    primal_sum, dual_sum = jnp.zeros_like(primal), jnp.zeros_like(dual)
    taken = jnp.zeros((1, LANES), jnp.float32)
    col_iota = lax.broadcasted_iota(jnp.int32, (blocks, LANES), 0)

    for turn in range(iters):
        slot = turn % 2
        last = turn == iters - 1
        if turn >= 2:
            grad_copy(slot).wait_send()
        dual_move = jnp.sum(moves, axis=1, keepdims=True)
        grad_out[slot, pl.ds(blocks, 8)] = jnp.broadcast_to(dual_move, (8, LANES))
        primal_move = jnp.sum(primal_moves, axis=1, keepdims=True)
        primal_root = jnp.sqrt(primal_move + EPSILON)
        parts = []
        for t in range(count):
            line = dual_all[pl.ds(rows_s[t], 1)]
            parts.append(jnp.where(col_iota == cols_s[t], line, 0.0).astype(jnp.bfloat16))
        left = jnp.concatenate(parts, axis=1)
        partial = jnp.dot(
            left, tiles[...].reshape(count * LANES, LANES), preferred_element_type=jnp.float32
        )
        grad_out[slot, pl.ds(0, blocks)] = partial
        grad_copy(slot).start()
        grad_copy(slot).wait_recv()
        gradient = partial + grad_in[slot, pl.ds(0, blocks)]
        if turn > 0:
            dual_move = dual_move + grad_in[slot, pl.ds(blocks, 1)]
            candidate = jnp.sqrt(weight * jnp.sqrt(dual_move + EPSILON) / primal_root)
            weight = jnp.where(flags_s[turn - 1] == 1, candidate, weight)
        restart = flags_s[turn] == 1
        primal_next = jnp.clip(primal - eta / weight * (cost + gradient), 0.0, bound)
        extrapolated = 2.0 * primal_next - primal
        primal_sum = primal_sum + primal_next
        taken = taken + 1.0
        primal_mean = primal_sum / taken
        shift = primal_mean - anchor_primal
        primal_part = jnp.sum(shift * shift, axis=0, keepdims=True)
        primal = jnp.where(restart, primal_mean, primal_next)
        anchor_primal = jnp.where(restart, primal_mean, anchor_primal)
        primal_sum = jnp.where(restart, 0.0, primal_sum)

        rows = 2 * own if last else own
        row_iota = lax.broadcasted_iota(jnp.int32, (n * rows, LANES), 0)
        parts = []
        lines = [extrapolated, primal] if last else [extrapolated]
        for index, line in enumerate(lines):
            flows[index] = line
        for t in range(count):
            row, col = rows_s[t], cols_s[t]
            spot = (row // own) * rows + row % own
            piece = jnp.zeros((n * rows, LANES), jnp.float32)
            for index in range(len(lines)):
                line = flows[index, pl.ds(col, 1)]
                piece = jnp.where(row_iota == spot + index * own, line, piece)
            parts.append(piece.astype(jnp.bfloat16))
        left = jnp.concatenate(parts, axis=1)
        activity = jnp.dot(
            left, turned[...].reshape(count * LANES, LANES), preferred_element_type=jnp.float32
        )
        if last:
            for q in range(n):
                act_out[q] = activity[q * rows : (q + 1) * rows]
            peers(lambda q: act_copy(me, q).start())
            act_in[me] = act_out[me]
            mine = pl.ds(me * own, own)
            dual = dual_all[mine]
            limit_all[...] = dual_sum
            dual_sum = limit_all[mine]
            peers(lambda q: act_copy(q, q).wait_recv())
            total = jnp.sum(act_in[...], axis=0)
            dual_next = jnp.maximum(dual + eta * weight * (total[:own] - dual_buf[me, pl.ds(own, own)]), 0.0)
            dual = jnp.where(restart, (dual_sum + dual_next) / taken, dual_next)
        else:
            if turn >= 2:
                peers(lambda q: all_copy(slot, me, q).wait_send())
            act_all[slot, me, pl.ds(0, n * own)] = activity
            act_all[slot, me, pl.ds(n * own, 1)] = primal_part
            peers(lambda q: all_copy(slot, me, q).start())
            peers(lambda q: all_copy(slot, q, q).wait_recv())
            total = jnp.sum(act_all[slot, :, pl.ds(0, n * own)], axis=0)
            primal_moves = jnp.sum(act_all[slot, :, n * own, :], axis=0, keepdims=True)
            dual_next = jnp.maximum(dual + eta * weight * (total - limits), 0.0)
            dual_sum = dual_sum + dual_next
            dual_mean = dual_sum / taken
            shift = dual_mean - anchor_dual
            moves = jnp.sum(shift * shift, axis=0, keepdims=True)
            dual = jnp.where(restart, dual_mean, dual_next)
            anchor_dual = jnp.where(restart, dual_mean, anchor_dual)
            dual_sum = jnp.where(restart, 0.0, dual_sum)
            taken = jnp.where(restart, 0.0, taken)
            dual_all[...] = dual

    primal_out[...] = jnp.where(core == 0, primal[:half], primal[half:])
    dual_out[...] = dual
    loads_out[...] = total[own:]
    peers(lambda q: act_copy(me, q).wait_send())
    for turn in range(max(iters - 3, 0), iters - 1):
        peers(functools.partial(lambda slot, q: all_copy(slot, me, q).wait_send(), turn % 2))
    for turn in range(max(iters - 2, 0), iters):
        grad_copy(turn % 2).wait_send()


def shards(
    tile_values,
    row_blocks,
    col_blocks,
    path_cost,
    path_bound,
    primal_start,
    dual_start,
    row_limits,
    step_size,
    weight_start,
    restart_flags,
):
    n = lax.axis_size("path")
    count = row_blocks.shape[2]
    half = path_cost.shape[0] // LANES
    own = dual_start.shape[0] // LANES
    vmem = pl.BlockSpec(memory_space=pltpu.VMEM)
    smem = pl.BlockSpec(memory_space=pltpu.SMEM)
    hbm = pl.BlockSpec(memory_space=pltpu.HBM)
    dma = pltpu.SemaphoreType.DMA
    primal, dual, loads = pl.pallas_call(
        functools.partial(kernel, n, restart_flags.shape[0]),
        out_shape=(
            jax.ShapeDtypeStruct((half, LANES), jnp.float32),
            jax.ShapeDtypeStruct((own, LANES), jnp.float32),
            jax.ShapeDtypeStruct((own, LANES), jnp.float32),
        ),
        in_specs=[
            hbm,
            smem,
            smem,
            hbm,
            hbm,
            hbm,
            hbm,
            hbm,
            smem,
            smem,
            smem,
        ],
        out_specs=(vmem, vmem, vmem),
        scratch_shapes=[
            pltpu.VMEM((count, LANES, LANES), jnp.bfloat16),
            pltpu.VMEM((count, LANES, LANES), jnp.bfloat16),
            pltpu.VMEM((2, 3, half, LANES), jnp.float32),
            pltpu.VMEM((2, 2 * half, LANES), jnp.float32),
            pltpu.VMEM((n, 2 * own, LANES), jnp.float32),
            pltpu.VMEM((n * own, LANES), jnp.float32),
            pltpu.VMEM((n * own, LANES), jnp.float32),
            pltpu.VMEM((2, 2 * half + 8, LANES), jnp.float32),
            pltpu.VMEM((2, 2 * half + 8, LANES), jnp.float32),
            pltpu.VMEM((2, n, n * own + 1, LANES), jnp.float32),
            pltpu.VMEM((n, 2 * own, LANES), jnp.float32),
            pltpu.VMEM((n, 2 * own, LANES), jnp.float32),
            dma,
            dma((5,)),
            dma,
            dma,
            dma((n,)),
            dma((n,)),
            dma((2,)),
            dma((2,)),
            dma((2, n)),
            dma((2, n)),
            dma((n,)),
            dma((n,)),
        ],
        compiler_params=pltpu.CompilerParams(
            collective_id=0, has_side_effects=True, vmem_limit_bytes=63 * 1024 * 1024
        ),
    )(
        tile_values,
        row_blocks.reshape(count),
        col_blocks.reshape(count),
        path_cost.reshape(half, LANES),
        path_bound.reshape(half, LANES),
        primal_start.reshape(half, LANES),
        dual_start.reshape(own, LANES),
        row_limits.reshape(own, LANES),
        step_size,
        weight_start,
        restart_flags,
    )
    return (primal.reshape(-1), dual.reshape(-1), loads.reshape(-1))


def solution(mesh):
    in_specs = (
        P(("groups", "path"), "cons", None, None, None),
        P(("groups", "path"), "cons", None),
        P(("groups", "path"), "cons", None),
        P(("groups", "path", "cons")),
        P(("groups", "path", "cons")),
        P(("groups", "path", "cons")),
        P(("groups", "path", "cons")),
        P(("groups", "path", "cons")),
        P("groups"),
        P("groups"),
        P("groups"),
    )
    out_specs = (
        P(("groups", "path", "cons")),
        P(("groups", "path", "cons")),
        P(("groups", "path", "cons")),
    )
    return jax.shard_map(shards, mesh=mesh, in_specs=in_specs, out_specs=out_specs, check_vma=False)
```

```python
import functools
import jax
import jax.numpy as jnp
from jax import lax
from jax.experimental import pallas as pl
from jax.experimental.pallas import tpu as pltpu
from jax.sharding import PartitionSpec as P

LANES = 128
EPSILON = 1e-06


def kernel(
    n,
    iters,
    tiles_hbm,
    rows_s,
    cols_s,
    cost_in,
    bound_in,
    primal_in,
    dual_in,
    limits_in,
    step_s,
    weight_s,
    flags_s,
    result,
    tiles,
    turned,
    start_buf,
    flows,
    dual_buf,
    dual_all,
    limit_all,
    grad_out,
    grad_in,
    act_all,
    act_out,
    act_in,
    tile_sem,
    fetch_sem,
    start_send,
    start_recv,
    dual_send,
    dual_recv,
    grad_send,
    grad_recv,
    all_send,
    all_recv,
    act_send,
    act_recv,
):
    me = lax.axis_index("path")
    core = lax.axis_index("cons")
    other = 1 - core
    count = tiles.shape[0]
    half = cost_in.shape[0]
    own = dual_in.shape[0]
    blocks = 2 * half
    unroll = n <= 8

    flips = []
    if n == 8:
        bits = [lax.rem(me // (1 << i), 2) for i in range(3)]
        for k in range(7, 0, -1):
            flips.append(me + sum((1 << i) * (1 - 2 * bits[i]) for i in range(3) if k >> i & 1))

    def peers(body):
        def step(k, carry):
            body(lax.rem(me + k, n))
            return carry

        if flips:
            for q in flips:
                body(q)
            return

        lax.fori_loop(1, n, step, 0, unroll=unroll)

    tile_copy = pltpu.make_async_copy(tiles_hbm.at[0, 0], tiles, tile_sem)
    fetches = [
        pltpu.make_async_copy(dual_in, dual_buf.at[me, pl.ds(0, own)], fetch_sem.at[0]),
        pltpu.make_async_copy(limits_in, dual_buf.at[me, pl.ds(own, own)], fetch_sem.at[1]),
        pltpu.make_async_copy(cost_in, start_buf.at[core, 0], fetch_sem.at[2]),
        pltpu.make_async_copy(bound_in, start_buf.at[core, 1], fetch_sem.at[3]),
        pltpu.make_async_copy(primal_in, start_buf.at[core, 2], fetch_sem.at[4]),
    ]
    for copy in fetches:
        copy.start()
    tile_copy.start()
    barrier = pltpu.get_barrier_semaphore()
    peers(lambda q: pl.semaphore_signal(barrier, inc=1, device_id={"path": q}))
    pl.semaphore_signal(barrier, inc=1, device_id={"cons": other})

    for copy in fetches:
        copy.wait()
    pl.semaphore_wait(barrier, n)

    def dual_copy(source, q):
        return pltpu.make_async_remote_copy(
            src_ref=dual_buf.at[source],
            dst_ref=dual_buf.at[source],
            send_sem=dual_send.at[q],
            recv_sem=dual_recv.at[source],
            device_id={"path": q},
        )

    def all_copy(slot, source, q):
        return pltpu.make_async_remote_copy(
            src_ref=act_all.at[slot, source],
            dst_ref=act_all.at[slot, source],
            send_sem=all_send.at[slot, q],
            recv_sem=all_recv.at[slot, source],
            device_id={"path": q},
        )

    def act_copy(source, q):
        return pltpu.make_async_remote_copy(
            src_ref=act_out.at[q],
            dst_ref=act_in.at[source],
            send_sem=act_send.at[q],
            recv_sem=act_recv.at[source],
            device_id={"path": q},
        )

    def grad_copy(slot):
        return pltpu.make_async_remote_copy(
            src_ref=grad_out.at[slot],
            dst_ref=grad_in.at[slot],
            send_sem=grad_send.at[slot],
            recv_sem=grad_recv.at[slot],
            device_id={"cons": other},
        )

    def start_copy(slot):
        return pltpu.make_async_remote_copy(
            src_ref=start_buf.at[slot],
            dst_ref=start_buf.at[slot],
            send_sem=start_send,
            recv_sem=start_recv,
            device_id={"cons": other},
        )

    peers(lambda q: dual_copy(me, q).start())
    start_copy(core).start()
    tile_copy.wait()
    for t in range(count):
        turned[t] = tiles[t].T
    start_copy(other).wait_recv()

    def whole(item):
        return jnp.concatenate([start_buf[0, item], start_buf[1, item]], axis=0)

    cost, bound, primal = whole(0), whole(1), whole(2)
    start_copy(core).wait_send()
    peers(lambda q: dual_copy(q, q).wait_recv())
    for q in range(n):
        dual_all[pl.ds(q * own, own)] = dual_buf[q, pl.ds(0, own)]
        limit_all[pl.ds(q * own, own)] = dual_buf[q, pl.ds(own, own)]
    dual = dual_all[...]
    limits = limit_all[...]
    peers(lambda q: dual_copy(me, q).wait_send())
    moves = jnp.zeros((1, LANES), jnp.float32)
    primal_moves = moves
    eta = step_s[0]
    weight = jnp.full((1, LANES), weight_s[0], jnp.float32)
    anchor_primal, anchor_dual = primal, dual
    primal_sum, dual_sum = jnp.zeros_like(primal), jnp.zeros_like(dual)
    taken = jnp.zeros((1, LANES), jnp.float32)
    col_iota = lax.broadcasted_iota(jnp.int32, (blocks, LANES), 0)

    for turn in range(iters):
        slot = turn % 2
        last = turn == iters - 1
        if turn >= 2:
            grad_copy(slot).wait_send()
        dual_move = jnp.sum(moves, axis=1, keepdims=True)
        grad_out[slot, pl.ds(blocks, 8)] = jnp.broadcast_to(dual_move, (8, LANES))
        primal_move = jnp.sum(primal_moves, axis=1, keepdims=True)
        primal_root = jnp.sqrt(primal_move + EPSILON)
        parts = []
        for t in range(count):
            line = dual_all[pl.ds(rows_s[t], 1)]
            parts.append(jnp.where(col_iota == cols_s[t], line, 0.0).astype(jnp.bfloat16))
        left = jnp.concatenate(parts, axis=1)
        partial = jnp.dot(
            left, tiles[...].reshape(count * LANES, LANES), preferred_element_type=jnp.float32
        )
        grad_out[slot, pl.ds(0, blocks)] = partial
        grad_copy(slot).start()
        grad_copy(slot).wait_recv()
        gradient = partial + grad_in[slot, pl.ds(0, blocks)]
        if turn > 0:
            dual_move = dual_move + grad_in[slot, pl.ds(blocks, 1)]
            candidate = jnp.sqrt(weight * jnp.sqrt(dual_move + EPSILON) / primal_root)
            weight = jnp.where(flags_s[turn - 1] == 1, candidate, weight)
        restart = flags_s[turn] == 1
        primal_next = jnp.clip(primal - eta / weight * (cost + gradient), 0.0, bound)
        extrapolated = 2.0 * primal_next - primal
        primal_sum = primal_sum + primal_next
        taken = taken + 1.0
        primal_mean = primal_sum / taken
        shift = primal_mean - anchor_primal
        primal_part = jnp.sum(shift * shift, axis=0, keepdims=True)
        primal = jnp.where(restart, primal_mean, primal_next)
        anchor_primal = jnp.where(restart, primal_mean, anchor_primal)
        primal_sum = jnp.where(restart, 0.0, primal_sum)

        rows = 2 * own if last else own
        row_iota = lax.broadcasted_iota(jnp.int32, (n * rows, LANES), 0)
        parts = []
        lines = [extrapolated, primal] if last else [extrapolated]
        for index, line in enumerate(lines):
            flows[index] = line
        for t in range(count):
            row, col = rows_s[t], cols_s[t]
            spot = (row // own) * rows + row % own
            piece = jnp.zeros((n * rows, LANES), jnp.float32)
            for index in range(len(lines)):
                line = flows[index, pl.ds(col, 1)]
                piece = jnp.where(row_iota == spot + index * own, line, piece)
            parts.append(piece.astype(jnp.bfloat16))
        left = jnp.concatenate(parts, axis=1)
        activity = jnp.dot(
            left, turned[...].reshape(count * LANES, LANES), preferred_element_type=jnp.float32
        )
        if last:
            for q in range(n):
                act_out[q] = activity[q * rows : (q + 1) * rows]
            peers(lambda q: act_copy(me, q).start())
            act_in[me] = act_out[me]
            mine = pl.ds(me * own, own)
            dual = dual_all[mine]
            limit_all[...] = dual_sum
            dual_sum = limit_all[mine]
            peers(lambda q: act_copy(q, q).wait_recv())
            total = jnp.sum(act_in[...], axis=0)
            dual_next = jnp.maximum(dual + eta * weight * (total[:own] - dual_buf[me, pl.ds(own, own)]), 0.0)
            dual = jnp.where(restart, (dual_sum + dual_next) / taken, dual_next)
        else:
            if turn >= 2:
                peers(lambda q: all_copy(slot, me, q).wait_send())
            act_all[slot, me, pl.ds(0, n * own)] = activity
            act_all[slot, me, pl.ds(n * own, 1)] = primal_part
            peers(lambda q: all_copy(slot, me, q).start())
            peers(lambda q: all_copy(slot, q, q).wait_recv())
            total = jnp.sum(act_all[slot, :, pl.ds(0, n * own)], axis=0)
            primal_moves = jnp.sum(act_all[slot, :, n * own, :], axis=0, keepdims=True)
            dual_next = jnp.maximum(dual + eta * weight * (total - limits), 0.0)
            dual_sum = dual_sum + dual_next
            dual_mean = dual_sum / taken
            shift = dual_mean - anchor_dual
            moves = jnp.sum(shift * shift, axis=0, keepdims=True)
            dual = jnp.where(restart, dual_mean, dual_next)
            anchor_dual = jnp.where(restart, dual_mean, anchor_dual)
            dual_sum = jnp.where(restart, 0.0, dual_sum)
            taken = jnp.where(restart, 0.0, taken)
            dual_all[...] = dual

    result[pl.ds(0, half)] = jnp.where(core == 0, primal[:half], primal[half:])
    result[pl.ds(half, own)] = dual
    result[pl.ds(half + own, own)] = total[own:]
    peers(lambda q: act_copy(me, q).wait_send())
    for turn in range(max(iters - 3, 0), iters - 1):
        peers(functools.partial(lambda slot, q: all_copy(slot, me, q).wait_send(), turn % 2))
    for turn in range(max(iters - 2, 0), iters):
        grad_copy(turn % 2).wait_send()


def shards(
    tile_values,
    row_blocks,
    col_blocks,
    path_cost,
    path_bound,
    primal_start,
    dual_start,
    row_limits,
    step_size,
    weight_start,
    restart_flags,
):
    n = lax.axis_size("path")
    count = row_blocks.shape[2]
    half = path_cost.shape[0] // LANES
    own = dual_start.shape[0] // LANES
    vmem = pl.BlockSpec(memory_space=pltpu.VMEM)
    smem = pl.BlockSpec(memory_space=pltpu.SMEM)
    hbm = pl.BlockSpec(memory_space=pltpu.HBM)
    dma = pltpu.SemaphoreType.DMA
    result = pl.pallas_call(
        functools.partial(kernel, n, restart_flags.shape[0]),
        out_shape=jax.ShapeDtypeStruct((half + 2 * own, LANES), jnp.float32),
        in_specs=[
            hbm,
            smem,
            smem,
            hbm,
            hbm,
            hbm,
            hbm,
            hbm,
            smem,
            smem,
            smem,
        ],
        out_specs=vmem,
        scratch_shapes=[
            pltpu.VMEM((count, LANES, LANES), jnp.bfloat16),
            pltpu.VMEM((count, LANES, LANES), jnp.bfloat16),
            pltpu.VMEM((2, 3, half, LANES), jnp.float32),
            pltpu.VMEM((2, 2 * half, LANES), jnp.float32),
            pltpu.VMEM((n, 2 * own, LANES), jnp.float32),
            pltpu.VMEM((n * own, LANES), jnp.float32),
            pltpu.VMEM((n * own, LANES), jnp.float32),
            pltpu.VMEM((2, 2 * half + 8, LANES), jnp.float32),
            pltpu.VMEM((2, 2 * half + 8, LANES), jnp.float32),
            pltpu.VMEM((2, n, n * own + 1, LANES), jnp.float32),
            pltpu.VMEM((n, 2 * own, LANES), jnp.float32),
            pltpu.VMEM((n, 2 * own, LANES), jnp.float32),
            dma,
            dma((5,)),
            dma,
            dma,
            dma((n,)),
            dma((n,)),
            dma((2,)),
            dma((2,)),
            dma((2, n)),
            dma((2, n)),
            dma((n,)),
            dma((n,)),
        ],
        compiler_params=pltpu.CompilerParams(
            collective_id=0, has_side_effects=True, vmem_limit_bytes=63 * 1024 * 1024
        ),
    )(
        tile_values,
        row_blocks.reshape(count),
        col_blocks.reshape(count),
        path_cost.reshape(half, LANES),
        path_bound.reshape(half, LANES),
        primal_start.reshape(half, LANES),
        dual_start.reshape(own, LANES),
        row_limits.reshape(own, LANES),
        step_size,
        weight_start,
        restart_flags,
    )
    flat = result.reshape(-1)
    first, second = half * LANES, (half + own) * LANES
    return (flat[:first], flat[first:second], flat[second:])


def solution(mesh):
    in_specs = (
        P(("groups", "path"), "cons", None, None, None),
        P(("groups", "path"), "cons", None),
        P(("groups", "path"), "cons", None),
        P(("groups", "path", "cons")),
        P(("groups", "path", "cons")),
        P(("groups", "path", "cons")),
        P(("groups", "path", "cons")),
        P(("groups", "path", "cons")),
        P("groups"),
        P("groups"),
        P("groups"),
    )
    out_specs = (
        P(("groups", "path", "cons")),
        P(("groups", "path", "cons")),
        P(("groups", "path", "cons")),
    )
    return jax.shard_map(shards, mesh=mesh, in_specs=in_specs, out_specs=out_specs, check_vma=False)
```
